32 devices in a mesh: energy: 16 (over z, y, x), slab: 2 (over core).
Axes of the slice: x: 2, y: 2, z: 4, core: 2. Of those that a mesh axis runs over, the one named last changes fastest.
Arguments:
- green_local: bfloat16 [32, 2, 2, 512, 512], P('energy', 'slab'), may hold values from -2.5 to 2.5
- coupling: bfloat16 [2, 512, 512], P('slab', 'energy'), may hold values from -0.21875 to 0.21875
- masks: int32 [2, 4, 4], P('slab'), may hold values 0 or 1
- incident: bfloat16 [32, 2, 512, 2, 128], P('energy', 'slab'), may hold values from -3 to 3
- energy_index: int32 [32], P('energy'), may hold values from 0 to 255
Outputs:
- wave_field: bfloat16 [32, 2, 512, 2, 128], P('energy', 'slab')
- outflow: bfloat16 [32, 2, 512, 2, 128], P('energy', 'slab')
- density: float32 [2, 512, 2, 512], P('slab', 'energy')
The draws below stay inside these ranges and needn't reach their ends.
All inputs are finite; a program needn't handle non-finite values. No bound on the sum of `masks` on one device may be relied on, other than what follows from the above.
Results may differ from the reference program's by a relative error of at most 0.027.
Values may be sent and summed in bfloat16 or wider, within the bound.
A program may use at most 64 MiB of HBM per device.

```python
import math
import jax
import jax.numpy as jnp
from jax import lax

M = 512
BLK = 128
MB = 4
MODES = 128
ENERGIES = 32
SLABS = 2


def draw_green_local(key, part):
    noise_key = jax.random.fold_in(key, 11)
    size_key = jax.random.fold_in(key, 12)
    angle_key = jax.random.fold_in(key, 13)
    full_shape = (ENERGIES, SLABS, 2, M, M)
    row_shape = (ENERGIES, SLABS, 1, M, 1)
    noise = jnp.clip(jax.random.normal(noise_key, full_shape, jnp.float32), -4.0, 4.0) * (0.5 / math.sqrt(M))
    amplitude = jnp.exp(jax.random.uniform(size_key, row_shape, jnp.float32, math.log(0.6), math.log(1.4)))
    angles = jax.random.uniform(angle_key, row_shape, jnp.float32, -math.pi, 0.0)
    diagonal = jnp.concatenate([jnp.cos(angles), jnp.sin(angles)], axis=2) * amplitude
    identity_matrix = jnp.eye(M, dtype=jnp.float32)
    result = noise + diagonal * identity_matrix
    return result.astype(jnp.bfloat16)


def plant(values, own_key, least, top_value):
    spot = [jax.random.randint(jax.random.fold_in(own_key, axis), (), 0, length) for axis, length in enumerate(values.shape)]
    longest = values.shape.index(max(values.shape))
    neighbour = spot[:longest] + [(spot[longest] + 1) % values.shape[longest]] + spot[longest + 1:]
    return values.at[tuple(spot)].set(least).at[tuple(neighbour)].set(top_value)


def block_scale(rng, extent, split, smallest, top_value):
    def one(dim, shards_of):
        steps = jax.random.uniform(jax.random.fold_in(jax.random.fold_in(rng, 6), dim), (shards_of,), jnp.float32, smallest / len(split), top_value / len(split))
        return jnp.repeat(jnp.exp(steps), extent[dim] // shards_of).reshape((-1,) + (1,) * (len(extent) - dim - 1))

    gain = one(*split[0])
    for cut in split[1:]:
        gain = gain * one(*cut)
    return gain


def normal_values(stream_key, extent, deviation, limit, cuts=(), kind=jnp.bfloat16):
    drawn = deviation * jax.random.normal(stream_key, extent, jnp.float32)
    if cuts:
        drawn = drawn * block_scale(stream_key, extent, cuts, -0.22, 0.18)
    return jnp.clip(drawn, -limit, limit).astype(kind)


def setup_inputs(seed: int = 0) -> dict:
    splits = jax.random.split(jax.random.key(seed), 6)
    green_local = draw_green_local(jax.random.fold_in(splits[5], 71), 0)
    coupling = normal_values(splits[1], (SLABS, M, M), (3 * M // 2) ** -0.5, 0.21875, ((0, 2), (1, 16)))
    masks = plant((jax.random.randint(splits[2], (SLABS, MB, MB), 0, 4) < 3).astype(jnp.int32), jax.random.fold_in(splits[2], 1), 0, 1)
    incident = normal_values(splits[3], (ENERGIES, SLABS, M, 2, MODES), 0.5, 3.0, ((0, 16), (1, 2)))
    energy_index = plant(jax.random.randint(splits[4], (ENERGIES,), 0, 256), jax.random.fold_in(splits[4], 1), 0, 255).astype(jnp.int32)
    return {"green_local": green_local, "coupling": coupling, "masks": masks, "incident": incident, "energy_index": energy_index}


def apply_green(green_block, vector):
    orbitals = green_block.shape[1]
    mode_count = vector.shape[2]
    product = jnp.dot(green_block.reshape(2 * orbitals, orbitals), vector.reshape(orbitals, 2 * mode_count), preferred_element_type=jnp.float32)
    product = product.reshape(2, orbitals, 2, mode_count)
    real_part = product[0, :, 0] - product[1, :, 1]
    imag_part = product[0, :, 1] + product[1, :, 0]
    return jnp.stack([real_part, imag_part], axis=1).astype(jnp.bfloat16)


def couple_forward(matrix, vector):
    orbitals = vector.shape[0]
    product = jnp.dot(matrix, vector.reshape(orbitals, -1), preferred_element_type=jnp.float32)
    return product.reshape(vector.shape)


def couple_back(matrix, vector):
    orbitals = vector.shape[0]
    product = lax.dot_general(matrix, vector.reshape(orbitals, -1), (((0,), (0,)), ((), ())), preferred_element_type=jnp.float32)
    return product.reshape(vector.shape)


def relax(green_block, source_here, left_term, matrix, right_wave):
    summed = source_here.astype(jnp.float32) + left_term.astype(jnp.float32) + couple_forward(matrix, right_wave)
    return apply_green(green_block, summed.astype(jnp.bfloat16))


def fermi(index_values, scale):
    exponent = (index_values.astype(jnp.float32) - 128.0) / 24.0
    return scale / (1.0 + jnp.exp(exponent))


def reference(green_local, coupling, masks, incident, energy_index):
    opened = jnp.repeat(jnp.repeat(masks, BLK, axis=1), BLK, axis=2)
    coupled = coupling * opened.astype(jnp.bfloat16)

    def one_energy(energy_item):
        green_here, source = energy_item
        first_waves = [apply_green(green_here[slab_index], source[slab_index]) for slab_index in range(SLABS)]
        zero_wave = jnp.zeros_like(first_waves[0])
        incoming = zero_wave
        left_terms = []
        for slab_index in range(SLABS):
            right_wave = first_waves[slab_index + 1] if slab_index + 1 < SLABS else zero_wave
            relaxed = relax(green_here[slab_index], source[slab_index], incoming, coupled[slab_index], right_wave)
            left_terms.append(incoming)
            incoming = couple_back(coupled[slab_index], relaxed).astype(jnp.bfloat16)
        final_waves = [zero_wave] * SLABS
        after = zero_wave
        for slab_index in reversed(range(SLABS)):
            after = relax(green_here[slab_index], source[slab_index], left_terms[slab_index], coupled[slab_index], after)
            final_waves[slab_index] = after
        outflow_list = [couple_back(coupled[slab_index], final_waves[slab_index]).astype(jnp.bfloat16) for slab_index in range(SLABS)]
        return jnp.stack(final_waves), jnp.stack(outflow_list)

    wave_field, outflow = lax.map(one_energy, (green_local, incident))
    weights = fermi(energy_index, 4.0 / (ENERGIES * MODES))

    def slab_density(slab_waves):
        scaled = (slab_waves.astype(jnp.float32) * weights[:, None, None, None]).astype(jnp.bfloat16)
        left_side = scaled.transpose(1, 0, 2, 3).reshape(M, -1)
        right_real = slab_waves.transpose(1, 0, 2, 3).reshape(M, -1)
        right_imag = jnp.stack([-slab_waves[:, :, 1], slab_waves[:, :, 0]], axis=2).transpose(1, 0, 2, 3).reshape(M, -1)
        real_part = lax.dot_general(left_side, right_real, (((1,), (1,)), ((), ())), preferred_element_type=jnp.float32)
        imag_part = lax.dot_general(left_side, right_imag, (((1,), (1,)), ((), ())), preferred_element_type=jnp.float32)
        return jnp.stack([real_part, imag_part], axis=1)

    density = lax.map(slab_density, wave_field.transpose(1, 0, 2, 3, 4))
    return (wave_field, outflow, density)
```

```python
import functools

import jax
import jax.numpy as jnp
from jax import lax
from jax.experimental import pallas as pl
from jax.experimental.pallas import tpu as pltpu
from jax.sharding import PartitionSpec as P

MESH = pl.DeviceIdType.MESH
BF16 = jnp.bfloat16
F32 = jnp.float32


def dot(a, b):
    return jnp.dot(a, b, preferred_element_type=F32)


def dot_nt(a, b):
    return lax.dot_general(a, b, (((1,), (1,)), ((), ())), preferred_element_type=F32)


def turned(x):
    half = x.shape[1] // 2
    return jnp.concatenate([-x[:, half:], x[:, :half]], axis=1)


def gather_orders(k):
    first = list(range(k - 1, -1, -1))
    return [first, first[:-2] + first[-2:][::-1]]


def scatter_orders(k):
    first = list(range(k))
    return [first, first[:2][::-1] + first[2:]]


def kernel(n, slabs, count, scale, index_ref, mask_ref, green_ref, source_ref, coupling_ref,
           wave_ref, outflow_ref, density_ref, s):
    k = n.bit_length() - 1
    rows, orbitals = coupling_ref.shape
    me = lax.axis_index("energy")
    slab = lax.axis_index("slab")
    bit = [(me // 2**b) % 2 for b in range(k)]
    partner = [me + (1 - 2 * bit[b]) * 2**b for b in range(k)]
    gathered = s["gathered"]
    gathered[tuple(bit[b] for b in range(k - 1, -1, -1))] = coupling_ref[...]

    barrier = pltpu.get_barrier_semaphore()
    for b in range(k):
        pl.semaphore_signal(barrier, inc=1, device_id={"energy": partner[b]}, device_id_type=MESH)

    @pl.when(slab > 0)
    def _():
        pl.semaphore_signal(barrier, inc=1, device_id={"slab": slab - 1}, device_id_type=MESH)

    @pl.when(slab < slabs - 1)
    def _():
        pl.semaphore_signal(barrier, inc=1, device_id={"slab": slab + 1}, device_id_type=MESH)

    neighbours = jnp.minimum(slab, 1) + jnp.minimum(slabs - 1 - slab, 1)
    pl.semaphore_wait(barrier, k + neighbours)

    def green(e, x):
        return (dot(green_ref[e, 0], x) + dot(green_ref[e, 1], turned(x))).astype(BF16)

    def slab_copy(name, e, src, target):
        return pltpu.make_async_remote_copy(
            src_ref=src.at[e], dst_ref=s[name].at[e],
            send_sem=s[name + "_send"].at[e], recv_sem=s[name + "_recv"].at[e],
            device_id={"slab": target}, device_id_type=MESH,
        )

    def start_copy(e):
        return slab_copy("start", e, s["first"], slab - 1)

    def flux_copy(e):
        return slab_copy("flux", e, s["flux_out"], slab + 1)

    def wave_copy(e):
        return slab_copy("right_wave", e, wave_ref, slab - 1)

    def gather_copy(h, i):
        order = gather_orders(k)[h]
        b = order[i]
        width = orbitals // 2
        place = tuple(slice(None) if c in order[:i] else bit[c] for c in range(k - 1, -1, -1))
        block = gathered.at[place + (slice(None), pl.ds(h * width, width))]
        return pltpu.make_async_remote_copy(
            src_ref=block, dst_ref=block,
            send_sem=s["gather_send"].at[h, i], recv_sem=s["gather_recv"].at[h, i],
            device_id={"energy": partner[b]}, device_id_type=MESH,
        )

    def scatter_place(h, i, own):
        order = scatter_orders(k)[h]
        left = [c for c in range(k - 1, -1, -1) if c not in order[:i]]
        b = order[i]
        return tuple((bit[c] if own else 1 - bit[c]) if c == b else slice(None) for c in left)

    def scatter_copy(h, i):
        b = scatter_orders(k)[h][i]
        return pltpu.make_async_remote_copy(
            src_ref=s["part"][h][i].at[scatter_place(h, i, False)], dst_ref=s["part_in"][h][i],
            send_sem=s["scatter_send"].at[h, i], recv_sem=s["scatter_recv"].at[h, i],
            device_id={"energy": partner[b]}, device_id_type=MESH,
        )

    for h in range(2):
        gather_copy(h, 0).start()

    @pl.when(slab > 0)
    def _():
        for e in range(count):
            s["first"][e] = green(e, source_ref[e])
            start_copy(e).start()

    for i in range(k):
        for h in range(2):
            gather_copy(h, i).wait_recv()
            if i + 1 < k:
                gather_copy(h, i + 1).start()

    whole = gathered[...].astype(F32).reshape(orbitals, orbitals)
    blocks = mask_ref.shape[0]
    tile = orbitals // blocks
    for i in range(blocks):
        for j in range(blocks):
            block = whole[i * tile:(i + 1) * tile, j * tile:(j + 1) * tile] * mask_ref[i, j].astype(F32)
            s["coupled"][i * tile:(i + 1) * tile, j * tile:(j + 1) * tile] = block.astype(BF16)
            s["coupled_t"][j * tile:(j + 1) * tile, i * tile:(i + 1) * tile] = block.T.astype(BF16)

    def sweep(has_left, has_right):
        for e in range(count):
            total = source_ref[e].astype(F32)
            if has_right:
                start_copy(e).wait_recv()
                total = total + dot(s["coupled"][...], s["start"][e])
            if has_left:
                flux_copy(e).wait_recv()
                total = total + s["flux"][e].astype(F32)
            forward = green(e, total.astype(BF16))
            if has_right:
                s["flux_out"][e] = dot(s["coupled_t"][...], forward).astype(BF16)
                flux_copy(e).start()
            else:
                wave_ref[e] = forward
                if has_left:
                    wave_copy(e).start()
        if has_right:
            for e in range(count):
                wave_copy(e).wait_recv()
                total = source_ref[e].astype(F32) + dot(s["coupled"][...], s["right_wave"][e])
                if has_left:
                    total = total + s["flux"][e].astype(F32)
                wave_ref[e] = green(e, total.astype(BF16))
                if has_left:
                    wave_copy(e).start()

    @pl.when(slab == 0)
    def _():
        sweep(False, slabs > 1)

    if slabs > 2:
        @pl.when((slab > 0) & (slab < slabs - 1))
        def _():
            sweep(True, True)

    if slabs > 1:
        @pl.when(slab == slabs - 1)
        def _():
            sweep(True, False)

    scaled = []
    for e in range(count):
        index = jnp.full((1, wave_ref.shape[2]), index_ref[e].astype(F32), F32)
        weight = scale / (1.0 + jnp.exp((index - 128.0) / 24.0))
        scaled.append((wave_ref[e].astype(F32) * weight).astype(BF16))
    left_side = jnp.concatenate(scaled, axis=1)
    for h in range(2):
        waves = [turned(wave_ref[e]) if h else wave_ref[e] for e in range(count)]
        part = dot_nt(left_side, jnp.concatenate(waves, axis=1))
        s["part"][h][0][...] = part.reshape((2,) * k + (rows, orbitals)).astype(BF16)
        scatter_copy(h, 0).start()

    for e in range(count):
        outflow_ref[e] = dot(s["coupled_t"][...], wave_ref[e]).astype(BF16)

    for i in range(k):
        for h in range(2):
            scatter_copy(h, i).wait_recv()
            total = s["part"][h][i][scatter_place(h, i, True)].astype(F32) + s["part_in"][h][i][...].astype(F32)
            if i + 1 < k:
                s["part"][h][i + 1][...] = total.astype(BF16)
                scatter_copy(h, i + 1).start()
            else:
                density_ref[:, h * orbitals:(h + 1) * orbitals] = total

    for h in range(2):
        for i in range(k):
            gather_copy(h, i).wait_send()
            scatter_copy(h, i).wait_send()

    @pl.when(slab > 0)
    def _():
        for e in range(count):
            start_copy(e).wait_send()
            wave_copy(e).wait_send()

    @pl.when(slab < slabs - 1)
    def _():
        for e in range(count):
            flux_copy(e).wait_send()


def shards(green_local, coupling, masks, incident, energy_index):
    count = green_local.shape[0]
    orbitals = green_local.shape[3]
    modes = incident.shape[4]
    rows = coupling.shape[1]
    slabs = lax.axis_size("slab")
    n = lax.axis_size("energy")
    k = n.bit_length() - 1
    wave = (count, orbitals, 2 * modes)
    scratch = {
        "gathered": pltpu.VMEM((2,) * k + (rows, orbitals), BF16),
        "coupled": pltpu.VMEM((orbitals, orbitals), BF16),
        "coupled_t": pltpu.VMEM((orbitals, orbitals), BF16),
        "first": pltpu.VMEM(wave, BF16),
        "flux_out": pltpu.VMEM(wave, BF16),
        "gather_send": pltpu.SemaphoreType.DMA((2, k)),
        "gather_recv": pltpu.SemaphoreType.DMA((2, k)),
        "scatter_send": pltpu.SemaphoreType.DMA((2, k)),
        "scatter_recv": pltpu.SemaphoreType.DMA((2, k)),
        "part": [[pltpu.VMEM((2,) * (k - i) + (rows, orbitals), BF16) for i in range(k)] for h in range(2)],
        "part_in": [[pltpu.VMEM((2,) * (k - i - 1) + (rows, orbitals), BF16) for i in range(k)] for h in range(2)],
    }
    for name in ("start", "flux", "right_wave"):
        scratch[name] = pltpu.VMEM(wave, BF16)
        scratch[name + "_send"] = pltpu.SemaphoreType.DMA((count,))
        scratch[name + "_recv"] = pltpu.SemaphoreType.DMA((count,))
    vmem = pl.BlockSpec(memory_space=pltpu.VMEM)
    smem = pl.BlockSpec(memory_space=pltpu.SMEM)
    wave_field, outflow, density = pl.pallas_call(
        functools.partial(kernel, n, slabs, count, 4.0 / (count * n * modes)),
        out_shape=(
            jax.ShapeDtypeStruct(wave, BF16),
            jax.ShapeDtypeStruct(wave, BF16),
            jax.ShapeDtypeStruct((rows, 2 * orbitals), F32),
        ),
        in_specs=[smem, smem, vmem, vmem, vmem],
        out_specs=(vmem, vmem, vmem),
        scratch_shapes=[scratch],
        compiler_params=pltpu.CompilerParams(
            collective_id=0, has_side_effects=True, vmem_limit_bytes=48 * 2**20
        ),
        name="sweep_and_density",
    )(energy_index, masks[0], green_local[:, 0], incident[:, 0].reshape(wave), coupling[0])
    shape = (count, 1, orbitals, 2, modes)
    return (wave_field.reshape(shape), outflow.reshape(shape), density.reshape(1, rows, 2, orbitals))


def solution(mesh):
    return jax.shard_map(
        shards,
        mesh=mesh,
        in_specs=(
            P("energy", "slab", None, None, None),
            P("slab", "energy", None),
            P("slab", None, None),
            P("energy", "slab", None, None, None),
            P("energy"),
        ),
        out_specs=(
            P("energy", "slab", None, None, None),
            P("energy", "slab", None, None, None),
            P("slab", "energy", None, None),
        ),
        check_vma=False,
    )
```

```python
import functools

import jax
import jax.numpy as jnp
from jax import lax
from jax.experimental import pallas as pl
from jax.experimental.pallas import tpu as pltpu
from jax.sharding import PartitionSpec as P

MESH = pl.DeviceIdType.MESH
BF16 = jnp.bfloat16
F32 = jnp.float32


def dot(a, b):
    return jnp.dot(a, b, preferred_element_type=F32)


def dot_nt(a, b):
    return lax.dot_general(a, b, (((1,), (1,)), ((), ())), preferred_element_type=F32)


def turned(x):
    half = x.shape[1] // 2
    return jnp.concatenate([-x[:, half:], x[:, :half]], axis=1)


def build(n, slabs, count, scale, index_hbm, mask_hbm, green_hbm, incident_hbm, coupling_hbm,
          wave_ref, outflow_ref, density_ref, s):
    layers = n // 4
    _, rows, orbitals = coupling_hbm.shape
    modes = incident_hbm.shape[4]
    me = lax.axis_index("energy")
    slab = lax.axis_index("slab")
    z, y, x = me // 4, (me // 2) % 2, me % 2
    across = {"x": me + 1 - 2 * x, "y": me + 2 - 4 * y}

    def layer_peer(j):
        return ((z + j) % layers) * 4 + me % 4

    gathered = s["gathered"]
    source_ref = s["source"]
    own = gathered.at[z, y, x]
    local = [pltpu.make_async_copy(coupling_hbm.at[0], own, s["local"].at[0])]
    local.append(pltpu.make_async_copy(incident_hbm.at[:, 0], s["raw"], s["local"].at[1]))
    local.append(pltpu.make_async_copy(index_hbm, s["index"], s["local"].at[2]))
    local.append(pltpu.make_async_copy(mask_hbm.at[0], s["mask"], s["local"].at[3]))
    for copy in local:
        copy.start()
    green_copies = []
    for e in range(count):
        for p in range(2):
            copy = pltpu.make_async_copy(
                green_hbm.at[e, 0, p], s["green"].at[e, :, pl.ds(p * orbitals, orbitals)], s["green_in"].at[e, p]
            )
            copy.start()
            green_copies.append(copy)

    barrier = pltpu.get_barrier_semaphore()
    for peer in [across["x"], across["y"]] + [layer_peer(j) for j in range(1, layers)]:
        pl.semaphore_signal(barrier, inc=1, device_id={"energy": peer}, device_id_type=MESH)

    @pl.when(slab > 0)
    def _():
        pl.semaphore_signal(barrier, inc=1, device_id={"slab": slab - 1}, device_id_type=MESH)

    @pl.when(slab < slabs - 1)
    def _():
        pl.semaphore_signal(barrier, inc=1, device_id={"slab": slab + 1}, device_id_type=MESH)

    local[1].wait()
    for e in range(count):
        source_ref[e] = jnp.concatenate([s["raw"][e, :, 0, :], s["raw"][e, :, 1, :]], axis=1)
    for copy in [local[0]] + local[2:] + green_copies:
        copy.wait()
    neighbours = jnp.minimum(slab, 1) + jnp.minimum(slabs - 1 - slab, 1)
    pl.semaphore_wait(barrier, layers + 1 + neighbours)

    def green(e, v):
        return dot(s["green"][e], jnp.concatenate([v, turned(v)], axis=0)).astype(BF16)

    def slab_copy(name, e, src, target):
        return pltpu.make_async_remote_copy(
            src_ref=src.at[e], dst_ref=s[name].at[e],
            send_sem=s[name + "_send"].at[e], recv_sem=s[name + "_recv"].at[e],
            device_id={"slab": target}, device_id_type=MESH,
        )

    def start_copy(e):
        return slab_copy("start", e, s["first"], slab - 1)

    def flux_copy(e):
        return slab_copy("flux", e, s["flux_out"], slab + 1)

    def wave_copy(e):
        return slab_copy("right_wave", e, wave_ref, slab - 1)

    def gather_layer(j):
        return pltpu.make_async_remote_copy(
            src_ref=own, dst_ref=own,
            send_sem=s["layer_send"].at[j], recv_sem=s["layer_recv"].at[j],
            device_id={"energy": layer_peer(j)}, device_id_type=MESH,
        )

    def gather_across(h, i):
        axis = ("yx", "xy")[h][i]
        columns = pl.ds(h * (orbitals // 2), orbitals // 2)
        yy = y if axis == "y" or i == 0 else slice(None)
        xx = x if axis == "x" or i == 0 else slice(None)
        block = gathered.at[:, yy, xx, :, columns]
        return pltpu.make_async_remote_copy(
            src_ref=block, dst_ref=block,
            send_sem=s["across_send"].at[h, i], recv_sem=s["across_recv"].at[h, i],
            device_id={"energy": across[axis]}, device_id_type=MESH,
        )

    def gather_0():
        for j in range(1, layers):
            gather_layer(j).start()

    def gather_1():
        for j in range(1, layers):
            gather_layer(j).wait_recv()
        for h in range(2):
            gather_across(h, 0).start()

    def gather_2():
        for h in range(2):
            gather_across(h, 0).wait_recv()
            gather_across(h, 1).start()

    def gather_3():
        for h in range(2):
            gather_across(h, 1).wait_recv()
        whole = gathered[...].astype(F32).reshape(orbitals, orbitals)
        blocks = s["mask"].shape[0]
        tile = orbitals // blocks
        for i in range(blocks):
            for j in range(blocks):
                block = whole[i * tile:(i + 1) * tile, j * tile:(j + 1) * tile] * s["mask"][i, j].astype(F32)
                s["coupled"][i * tile:(i + 1) * tile, j * tile:(j + 1) * tile] = block.astype(BF16)

    def transpose_coupled():
        s["coupled_t"][...] = s["coupled"][...].T

    def send_first():
        for e in range(count):
            s["first"][e] = green(e, source_ref[e])
            start_copy(e).start()

    def sweep(has_left):
        gather_0()
        if has_left:
            send_first()
        gather_1()
        gather_2()
        gather_3()
        for e in range(count):
            start_copy(e).wait_recv()
            total = source_ref[e].astype(F32) + dot(s["coupled"][...], s["start"][e])
            if has_left:
                flux_copy(e).wait_recv()
                total = total + s["flux"][e].astype(F32)
            forward = green(e, total.astype(BF16))
            if e == 0:
                transpose_coupled()
            s["flux_out"][e] = dot(s["coupled_t"][...], forward).astype(BF16)
            flux_copy(e).start()
        for e in range(count):
            wave_copy(e).wait_recv()
            total = source_ref[e].astype(F32) + dot(s["coupled"][...], s["right_wave"][e])
            if has_left:
                total = total + s["flux"][e].astype(F32)
            wave_ref[e] = green(e, total.astype(BF16))
            if has_left:
                wave_copy(e).start()

    def last_sweep():
        send_first()
        for e in range(count):
            flux_copy(e).wait_recv()
            if e == 0:
                gather_0()
            total = source_ref[e].astype(F32) + s["flux"][e].astype(F32)
            wave_ref[e] = green(e, total.astype(BF16))
            wave_copy(e).start()
            if e == 0:
                gather_1()
        gather_2()

    @pl.when(slab == 0)
    def _():
        sweep(False)

    if slabs > 2:
        @pl.when((slab > 0) & (slab < slabs - 1))
        def _():
            sweep(True)

    @pl.when(slab == slabs - 1)
    def _():
        last_sweep()

    chunks = 4
    width = 2 * orbitals // chunks

    def scatter_axis(c, i):
        return ("xy", "yx")[c % 2][i]

    def scatter_place(c, i, keep):
        axis = scatter_axis(c, i)
        here = (x if axis == "x" else y) if keep else (1 - x if axis == "x" else 1 - y)
        if i == 1:
            return (slice(None), here)
        return (slice(None), slice(None), here) if axis == "x" else (slice(None), here)

    def scatter_across(c, i):
        return pltpu.make_async_remote_copy(
            src_ref=s["part"][c][i].at[scatter_place(c, i, False)], dst_ref=s["part_in"][c][i],
            send_sem=s["scatter_send"].at[c, i], recv_sem=s["scatter_recv"].at[c, i],
            device_id={"energy": across[scatter_axis(c, i)]}, device_id_type=MESH,
        )

    def scatter_layer(c, j):
        return pltpu.make_async_remote_copy(
            src_ref=s["part"][c][2].at[(z + j) % layers], dst_ref=s["part_in"][c][2].at[j],
            send_sem=s["final_send"].at[c, j], recv_sem=s["final_recv"].at[c, j],
            device_id={"energy": layer_peer(j)}, device_id_type=MESH,
        )

    scaled = []
    for e in range(count):
        index = jnp.full((1, 2 * modes), s["index"][e].astype(F32), F32)
        weight = scale / (1.0 + jnp.exp((index - 128.0) / 24.0))
        scaled.append((wave_ref[e].astype(F32) * weight).astype(BF16))
    left_side = jnp.concatenate(scaled, axis=1)
    for c in range(chunks):
        imag, quarter = c % 2, c // 2
        span = slice(quarter * width, (quarter + 1) * width)
        waves = [turned(wave_ref[e, span, :]) if imag else wave_ref[e, span, :] for e in range(count)]
        part = dot_nt(left_side, jnp.concatenate(waves, axis=1))
        s["part"][c][0][...] = part.reshape(layers, 2, 2, rows, width).astype(BF16)
        scatter_across(c, 0).start()

    @pl.when(slab == slabs - 1)
    def _():
        gather_3()
        transpose_coupled()

    for e in range(count):
        outflow_ref[e] = dot(s["coupled_t"][...], wave_ref[e]).astype(BF16)

    for i in range(2):
        for c in range(chunks):
            scatter_across(c, i).wait_recv()
            total = s["part"][c][i][scatter_place(c, i, True)].astype(F32) + s["part_in"][c][i][...].astype(F32)
            s["part"][c][i + 1][...] = total.astype(BF16)
            if i == 0:
                scatter_across(c, 1).start()
            else:
                for j in range(1, layers):
                    scatter_layer(c, j).start()
    for c in range(chunks):
        imag, quarter = c % 2, c // 2
        total = s["part"][c][2][z].astype(F32)
        for j in range(1, layers):
            scatter_layer(c, j).wait_recv()
            total = total + s["part_in"][c][2][j].astype(F32)
        begin = imag * orbitals + quarter * width
        density_ref[:, begin:begin + width] = total

    for j in range(1, layers):
        gather_layer(j).wait_send()
        for c in range(chunks):
            scatter_layer(c, j).wait_send()
    for i in range(2):
        for h in range(2):
            gather_across(h, i).wait_send()
        for c in range(chunks):
            scatter_across(c, i).wait_send()

    @pl.when(slab > 0)
    def _():
        for e in range(count):
            start_copy(e).wait_send()
            wave_copy(e).wait_send()

    @pl.when(slab < slabs - 1)
    def _():
        for e in range(count):
            flux_copy(e).wait_send()


def shards(green_local, coupling, masks, incident, energy_index):
    count = green_local.shape[0]
    orbitals = green_local.shape[3]
    modes = incident.shape[4]
    rows = coupling.shape[1]
    slabs = lax.axis_size("slab")
    n = lax.axis_size("energy")
    layers = n // 4
    chunks = 4
    width = 2 * orbitals // chunks
    wave = (count, orbitals, 2 * modes)
    dma = pltpu.SemaphoreType.DMA
    scratch = {
        "gathered": pltpu.VMEM((layers, 2, 2, rows, orbitals), BF16),
        "raw": pltpu.VMEM((count, orbitals, 2, modes), BF16),
        "source": pltpu.VMEM(wave, BF16),
        "index": pltpu.SMEM((count,), jnp.int32),
        "mask": pltpu.SMEM(masks.shape[1:], jnp.int32),
        "green": pltpu.VMEM((count, orbitals, 2 * orbitals), BF16),
        "coupled": pltpu.VMEM((orbitals, orbitals), BF16),
        "coupled_t": pltpu.VMEM((orbitals, orbitals), BF16),
        "first": pltpu.VMEM(wave, BF16),
        "flux_out": pltpu.VMEM(wave, BF16),
        "part": [[pltpu.VMEM((layers,) + (2,) * (2 - i) + (rows, width), BF16) for i in range(3)] for c in range(chunks)],
        "part_in": [[pltpu.VMEM((layers,) + (2,) * max(1 - i, 0) + (rows, width), BF16) for i in range(3)] for c in range(chunks)],
        "local": dma((4,)),
        "green_in": dma((count, 2)),
        "layer_send": dma((layers,)),
        "layer_recv": dma((layers,)),
        "across_send": dma((2, 2)),
        "across_recv": dma((2, 2)),
        "scatter_send": dma((chunks, 2)),
        "scatter_recv": dma((chunks, 2)),
        "final_send": dma((chunks, layers)),
        "final_recv": dma((chunks, layers)),
    }
    for name in ("start", "flux", "right_wave"):
        scratch[name] = pltpu.VMEM(wave, BF16)
        scratch[name + "_send"] = dma((count,))
        scratch[name + "_recv"] = dma((count,))
    vmem = pl.BlockSpec(memory_space=pltpu.VMEM)
    hbm = pl.BlockSpec(memory_space=pltpu.HBM)
    wave_field, outflow, density = pl.pallas_call(
        functools.partial(build, n, slabs, count, 4.0 / (count * n * modes)),
        out_shape=(
            jax.ShapeDtypeStruct(wave, BF16),
            jax.ShapeDtypeStruct(wave, BF16),
            jax.ShapeDtypeStruct((rows, 2 * orbitals), F32),
        ),
        in_specs=[hbm] * 5,
        out_specs=(vmem, vmem, vmem),
        scratch_shapes=[scratch],
        compiler_params=pltpu.CompilerParams(
            collective_id=0, has_side_effects=True, vmem_limit_bytes=60 * 2**20
        ),
        name="sweep_and_density",
    )(energy_index, masks, green_local, incident, coupling)
    shape = (count, 1, orbitals, 2, modes)
    return (wave_field.reshape(shape), outflow.reshape(shape), density.reshape(1, rows, 2, orbitals))


def solution(mesh):
    return jax.shard_map(
        shards,
        mesh=mesh,
        in_specs=(
            P("energy", "slab", None, None, None),
            P("slab", "energy", None),
            P("slab", None, None),
            P("energy", "slab", None, None, None),
            P("energy"),
        ),
        out_specs=(
            P("energy", "slab", None, None, None),
            P("energy", "slab", None, None, None),
            P("slab", "energy", None, None),
        ),
        check_vma=False,
    )
```

```python
import functools

import jax
import jax.numpy as jnp
from jax import lax
from jax.experimental import pallas as pl
from jax.experimental.pallas import tpu as pltpu
from jax.sharding import PartitionSpec as P

MESH = pl.DeviceIdType.MESH
BF16 = jnp.bfloat16
F32 = jnp.float32


def dot(a, b):
    return jnp.dot(a, b, preferred_element_type=F32)


def dot_nt(a, b):
    return lax.dot_general(a, b, (((1,), (1,)), ((), ())), preferred_element_type=F32)


def turned(x):
    half = x.shape[1] // 2
    return jnp.concatenate([-x[:, half:], x[:, :half]], axis=1)


def build(n, slabs, count, scale, index_hbm, mask_hbm, green_hbm, incident_hbm, coupling_hbm,
          wave_ref, outflow_ref, density_ref, s):
    layers = n // 4
    _, rows, orbitals = coupling_hbm.shape
    modes = incident_hbm.shape[4]
    me = lax.axis_index("energy")
    slab = lax.axis_index("slab")
    z, y, x = me // 4, (me // 2) % 2, me % 2
    across = {"x": me + 1 - 2 * x, "y": me + 2 - 4 * y}

    def layer_peer(j):
        return ((z + j) % layers) * 4 + me % 4

    gathered = s["gathered"]
    source_ref = s["source"]
    own = gathered.at[z, y, x]
    local = [pltpu.make_async_copy(coupling_hbm.at[0], own, s["local"].at[0])]
    local.append(pltpu.make_async_copy(incident_hbm.at[:, 0], s["raw"], s["local"].at[1]))
    local.append(pltpu.make_async_copy(index_hbm, s["index"], s["local"].at[2]))
    local.append(pltpu.make_async_copy(mask_hbm.at[0], s["mask"], s["local"].at[3]))
    for copy in local:
        copy.start()
    green_copies = []
    for e in range(count):
        for p in range(2):
            copy = pltpu.make_async_copy(
                green_hbm.at[e, 0, p], s["green"].at[e, :, pl.ds(p * orbitals, orbitals)], s["green_in"].at[e, p]
            )
            copy.start()
            green_copies.append(copy)

    barrier = pltpu.get_barrier_semaphore()
    for peer in [across["x"], across["y"]] + [layer_peer(j) for j in range(1, layers)]:
        pl.semaphore_signal(barrier, inc=1, device_id={"energy": peer}, device_id_type=MESH)

    @pl.when(slab > 0)
    def _():
        pl.semaphore_signal(barrier, inc=1, device_id={"slab": slab - 1}, device_id_type=MESH)

    @pl.when(slab < slabs - 1)
    def _():
        pl.semaphore_signal(barrier, inc=1, device_id={"slab": slab + 1}, device_id_type=MESH)

    local[0].wait()
    neighbours = jnp.minimum(slab, 1) + jnp.minimum(slabs - 1 - slab, 1)
    pl.semaphore_wait(barrier, layers + 1 + neighbours)

    def load():
        for copy in local[1:]:
            copy.wait()
        for e in range(count):
            source_ref[e] = jnp.concatenate([s["raw"][e, :, 0, :], s["raw"][e, :, 1, :]], axis=1)
        for copy in green_copies:
            copy.wait()

    def green(e, v):
        return dot(s["green"][e], jnp.concatenate([v, turned(v)], axis=0)).astype(BF16)

    def slab_copy(name, e, src, target):
        return pltpu.make_async_remote_copy(
            src_ref=src.at[e], dst_ref=s[name].at[e],
            send_sem=s[name + "_send"].at[e], recv_sem=s[name + "_recv"].at[e],
            device_id={"slab": target}, device_id_type=MESH,
        )

    def start_copy(e):
        return slab_copy("start", e, s["first"], slab - 1)

    def flux_copy(e):
        return slab_copy("flux", e, s["flux_out"], slab + 1)

    def wave_copy(e):
        return slab_copy("right_wave", e, wave_ref, slab - 1)

    def gather_layer(j):
        return pltpu.make_async_remote_copy(
            src_ref=own, dst_ref=own,
            send_sem=s["layer_send"].at[j], recv_sem=s["layer_recv"].at[j],
            device_id={"energy": layer_peer(j)}, device_id_type=MESH,
        )

    def gather_across(h, i):
        axis = ("yx", "xy")[h][i]
        columns = pl.ds(h * (orbitals // 2), orbitals // 2)
        yy = y if axis == "y" or i == 0 else slice(None)
        xx = x if axis == "x" or i == 0 else slice(None)
        block = gathered.at[:, yy, xx, :, columns]
        return pltpu.make_async_remote_copy(
            src_ref=block, dst_ref=block,
            send_sem=s["across_send"].at[h, i], recv_sem=s["across_recv"].at[h, i],
            device_id={"energy": across[axis]}, device_id_type=MESH,
        )

    def gather_0():
        for j in range(1, layers):
            gather_layer(j).start()

    def gather_1():
        for j in range(1, layers):
            gather_layer(j).wait_recv()
        for h in range(2):
            gather_across(h, 0).start()

    def gather_2():
        for h in range(2):
            gather_across(h, 0).wait_recv()
            gather_across(h, 1).start()

    def gather_3():
        for h in range(2):
            gather_across(h, 1).wait_recv()
        whole = gathered[...].astype(F32).reshape(orbitals, orbitals)
        blocks = s["mask"].shape[0]
        tile = orbitals // blocks
        for i in range(blocks):
            for j in range(blocks):
                block = whole[i * tile:(i + 1) * tile, j * tile:(j + 1) * tile] * s["mask"][i, j].astype(F32)
                s["coupled"][i * tile:(i + 1) * tile, j * tile:(j + 1) * tile] = block.astype(BF16)

    def transpose_coupled():
        s["coupled_t"][...] = s["coupled"][...].T

    def send_first():
        for e in range(count):
            s["first"][e] = green(e, source_ref[e])
            start_copy(e).start()

    def sweep(has_left):
        gather_0()
        if has_left:
            load()
            send_first()
        gather_1()
        if not has_left:
            load()
        gather_2()
        gather_3()
        for e in range(count):
            start_copy(e).wait_recv()
            total = source_ref[e].astype(F32) + dot(s["coupled"][...], s["start"][e])
            if has_left:
                flux_copy(e).wait_recv()
                total = total + s["flux"][e].astype(F32)
            forward = green(e, total.astype(BF16))
            if e == 0:
                transpose_coupled()
            s["flux_out"][e] = dot(s["coupled_t"][...], forward).astype(BF16)
            flux_copy(e).start()
        for e in range(count):
            wave_copy(e).wait_recv()
            total = source_ref[e].astype(F32) + dot(s["coupled"][...], s["right_wave"][e])
            if has_left:
                total = total + s["flux"][e].astype(F32)
            wave_ref[e] = green(e, total.astype(BF16))
            if has_left:
                wave_copy(e).start()

    def last_sweep():
        load()
        send_first()
        for e in range(count):
            flux_copy(e).wait_recv()
            if e == 0:
                gather_0()
            total = source_ref[e].astype(F32) + s["flux"][e].astype(F32)
            wave_ref[e] = green(e, total.astype(BF16))
            wave_copy(e).start()
            if e == 0:
                gather_1()
        gather_2()

    @pl.when(slab == 0)
    def _():
        sweep(False)

    if slabs > 2:
        @pl.when((slab > 0) & (slab < slabs - 1))
        def _():
            sweep(True)

    @pl.when(slab == slabs - 1)
    def _():
        last_sweep()

    chunks = 4
    width = 2 * orbitals // chunks

    def scatter_axis(c, i):
        return ("xy", "yx")[c % 2][i]

    def scatter_place(c, i, keep):
        axis = scatter_axis(c, i)
        here = (x if axis == "x" else y) if keep else (1 - x if axis == "x" else 1 - y)
        if i == 1:
            return (slice(None), here)
        return (slice(None), slice(None), here) if axis == "x" else (slice(None), here)

    def scatter_across(c, i):
        return pltpu.make_async_remote_copy(
            src_ref=s["part"][c][i].at[scatter_place(c, i, False)], dst_ref=s["part_in"][c][i],
            send_sem=s["scatter_send"].at[c, i], recv_sem=s["scatter_recv"].at[c, i],
            device_id={"energy": across[scatter_axis(c, i)]}, device_id_type=MESH,
        )

    def scatter_layer(c, j):
        return pltpu.make_async_remote_copy(
            src_ref=s["part"][c][2].at[(z + j) % layers], dst_ref=s["part_in"][c][2].at[j],
            send_sem=s["final_send"].at[c, j], recv_sem=s["final_recv"].at[c, j],
            device_id={"energy": layer_peer(j)}, device_id_type=MESH,
        )

    scaled = []
    for e in range(count):
        index = jnp.full((1, 2 * modes), s["index"][e].astype(F32), F32)
        weight = scale / (1.0 + jnp.exp((index - 128.0) / 24.0))
        scaled.append((wave_ref[e].astype(F32) * weight).astype(BF16))
    left_side = jnp.concatenate(scaled, axis=1)
    for c in range(chunks):
        imag, quarter = c % 2, c // 2
        span = slice(quarter * width, (quarter + 1) * width)
        waves = [turned(wave_ref[e, span, :]) if imag else wave_ref[e, span, :] for e in range(count)]
        part = dot_nt(left_side, jnp.concatenate(waves, axis=1))
        s["part"][c][0][...] = part.reshape(layers, 2, 2, rows, width).astype(BF16)
        scatter_across(c, 0).start()

    @pl.when(slab == slabs - 1)
    def _():
        gather_3()
        transpose_coupled()

    for e in range(count):
        outflow_ref[e] = dot(s["coupled_t"][...], wave_ref[e]).astype(BF16)

    for i in range(2):
        for c in range(chunks):
            scatter_across(c, i).wait_recv()
            total = s["part"][c][i][scatter_place(c, i, True)].astype(F32) + s["part_in"][c][i][...].astype(F32)
            s["part"][c][i + 1][...] = total.astype(BF16)
            if i == 0:
                scatter_across(c, 1).start()
            else:
                for j in range(1, layers):
                    scatter_layer(c, j).start()
    for c in range(chunks):
        imag, quarter = c % 2, c // 2
        total = s["part"][c][2][z].astype(F32)
        for j in range(1, layers):
            scatter_layer(c, j).wait_recv()
            total = total + s["part_in"][c][2][j].astype(F32)
        begin = imag * orbitals + quarter * width
        density_ref[:, begin:begin + width] = total

    for j in range(1, layers):
        gather_layer(j).wait_send()
        for c in range(chunks):
            scatter_layer(c, j).wait_send()
    for i in range(2):
        for h in range(2):
            gather_across(h, i).wait_send()
        for c in range(chunks):
            scatter_across(c, i).wait_send()

    @pl.when(slab > 0)
    def _():
        for e in range(count):
            start_copy(e).wait_send()
            wave_copy(e).wait_send()

    @pl.when(slab < slabs - 1)
    def _():
        for e in range(count):
            flux_copy(e).wait_send()


def shards(green_local, coupling, masks, incident, energy_index):
    count = green_local.shape[0]
    orbitals = green_local.shape[3]
    modes = incident.shape[4]
    rows = coupling.shape[1]
    slabs = lax.axis_size("slab")
    n = lax.axis_size("energy")
    layers = n // 4
    chunks = 4
    width = 2 * orbitals // chunks
    wave = (count, orbitals, 2 * modes)
    dma = pltpu.SemaphoreType.DMA
    scratch = {
        "gathered": pltpu.VMEM((layers, 2, 2, rows, orbitals), BF16),
        "raw": pltpu.VMEM((count, orbitals, 2, modes), BF16),
        "source": pltpu.VMEM(wave, BF16),
        "index": pltpu.SMEM((count,), jnp.int32),
        "mask": pltpu.SMEM(masks.shape[1:], jnp.int32),
        "green": pltpu.VMEM((count, orbitals, 2 * orbitals), BF16),
        "coupled": pltpu.VMEM((orbitals, orbitals), BF16),
        "coupled_t": pltpu.VMEM((orbitals, orbitals), BF16),
        "first": pltpu.VMEM(wave, BF16),
        "flux_out": pltpu.VMEM(wave, BF16),
        "part": [[pltpu.VMEM((layers,) + (2,) * (2 - i) + (rows, width), BF16) for i in range(3)] for c in range(chunks)],
        "part_in": [[pltpu.VMEM((layers,) + (2,) * max(1 - i, 0) + (rows, width), BF16) for i in range(3)] for c in range(chunks)],
        "local": dma((4,)),
        "green_in": dma((count, 2)),
        "layer_send": dma((layers,)),
        "layer_recv": dma((layers,)),
        "across_send": dma((2, 2)),
        "across_recv": dma((2, 2)),
        "scatter_send": dma((chunks, 2)),
        "scatter_recv": dma((chunks, 2)),
        "final_send": dma((chunks, layers)),
        "final_recv": dma((chunks, layers)),
    }
    for name in ("start", "flux", "right_wave"):
        scratch[name] = pltpu.VMEM(wave, BF16)
        scratch[name + "_send"] = dma((count,))
        scratch[name + "_recv"] = dma((count,))
    vmem = pl.BlockSpec(memory_space=pltpu.VMEM)
    hbm = pl.BlockSpec(memory_space=pltpu.HBM)
    wave_field, outflow, density = pl.pallas_call(
        functools.partial(build, n, slabs, count, 4.0 / (count * n * modes)),
        out_shape=(
            pltpu.VMEM(wave, BF16),
            pltpu.VMEM(wave, BF16),
            pltpu.VMEM((rows, 2 * orbitals), F32),
        ),
        in_specs=[hbm] * 5,
        out_specs=(vmem, vmem, vmem),
        scratch_shapes=[scratch],
        compiler_params=pltpu.CompilerParams(
            collective_id=0, has_side_effects=True, vmem_limit_bytes=60 * 2**20
        ),
        name="sweep_and_density",
    )(energy_index, masks, green_local, incident, coupling)
    shape = (count, 1, orbitals, 2, modes)
    return (wave_field.reshape(shape), outflow.reshape(shape), density.reshape(1, rows, 2, orbitals))


def solution(mesh):
    return jax.shard_map(
        shards,
        mesh=mesh,
        in_specs=(
            P("energy", "slab", None, None, None),
            P("slab", "energy", None),
            P("slab", None, None),
            P("energy", "slab", None, None, None),
            P("energy"),
        ),
        out_specs=(
            P("energy", "slab", None, None, None),
            P("energy", "slab", None, None, None),
            P("slab", "energy", None, None),
        ),
        check_vma=False,
    )
```

```python
import functools

import jax
import jax.numpy as jnp
from jax import lax
from jax.experimental import pallas as pl
from jax.experimental.pallas import tpu as pltpu
from jax.sharding import PartitionSpec as P

MESH = pl.DeviceIdType.MESH
BF16 = jnp.bfloat16
F32 = jnp.float32


def dot(a, b):
    return jnp.dot(a, b, preferred_element_type=F32)


def dot_nt(a, b):
    return lax.dot_general(a, b, (((1,), (1,)), ((), ())), preferred_element_type=F32)


def turned(x):
    half = x.shape[1] // 2
    return jnp.concatenate([-x[:, half:], x[:, :half]], axis=1)


PIECES = 4


class Group:
    def __init__(self, copies):
        self.copies = copies

    def start(self):
        for copy in self.copies:
            copy.start()

    def wait_recv(self):
        for copy in self.copies:
            copy.wait_recv()

    def wait_send(self):
        for copy in self.copies:
            copy.wait_send()


def build(n, slabs, count, scale, index_hbm, mask_hbm, green_hbm, incident_hbm, coupling_hbm,
          wave_ref, outflow_ref, density_ref, s):
    layers = n // 4
    _, rows, orbitals = coupling_hbm.shape
    modes = incident_hbm.shape[4]
    me = lax.axis_index("energy")
    slab = lax.axis_index("slab")
    z, y, x = me // 4, (me // 2) % 2, me % 2
    across = {"x": me + 1 - 2 * x, "y": me + 2 - 4 * y}

    def layer_peer(j):
        return ((z + j) % layers) * 4 + me % 4

    gathered = s["gathered"]
    source_ref = s["source"]
    own = gathered.at[z, y, x]
    local = [pltpu.make_async_copy(coupling_hbm.at[0], own, s["local"].at[0])]
    local.append(pltpu.make_async_copy(incident_hbm.at[:, 0], s["raw"], s["local"].at[1]))
    local.append(pltpu.make_async_copy(index_hbm, s["index"], s["local"].at[2]))
    local.append(pltpu.make_async_copy(mask_hbm.at[0], s["mask"], s["local"].at[3]))
    for copy in local:
        copy.start()
    green_copies = []
    for e in range(count):
        for p in range(2):
            copy = pltpu.make_async_copy(
                green_hbm.at[e, 0, p], s["green"].at[e, :, pl.ds(p * orbitals, orbitals)], s["green_in"].at[e, p]
            )
            copy.start()
            green_copies.append(copy)

    barrier = pltpu.get_barrier_semaphore()
    for peer in [across["x"], across["y"]] + [layer_peer(j) for j in range(1, layers)]:
        pl.semaphore_signal(barrier, inc=1, device_id={"energy": peer}, device_id_type=MESH)

    @pl.when(slab > 0)
    def _():
        pl.semaphore_signal(barrier, inc=1, device_id={"slab": slab - 1}, device_id_type=MESH)

    @pl.when(slab < slabs - 1)
    def _():
        pl.semaphore_signal(barrier, inc=1, device_id={"slab": slab + 1}, device_id_type=MESH)

    local[0].wait()
    neighbours = jnp.minimum(slab, 1) + jnp.minimum(slabs - 1 - slab, 1)
    pl.semaphore_wait(barrier, layers + 1 + neighbours)

    def load(energies):
        if 0 in energies:
            for copy in local[1:]:
                copy.wait()
        for e in energies:
            source_ref[e] = jnp.concatenate([s["raw"][e, :, 0, :], s["raw"][e, :, 1, :]], axis=1)
            for p in range(2):
                green_copies[2 * e + p].wait()

    def green(e, v):
        return dot(s["green"][e], jnp.concatenate([v, turned(v)], axis=0)).astype(BF16)

    def slab_copy(name, e, src, target):
        height = orbitals // PIECES
        copies = []
        for q in range(PIECES):
            span = pl.ds(q * height, height)
            copies.append(pltpu.make_async_remote_copy(
                src_ref=src.at[e, span], dst_ref=s[name].at[e, span],
                send_sem=s[name + "_send"].at[e, q], recv_sem=s[name + "_recv"].at[e, q],
                device_id={"slab": target}, device_id_type=MESH,
            ))
        return Group(copies)

    def start_copy(e):
        return slab_copy("start", e, s["first"], slab - 1)

    def flux_copy(e):
        return slab_copy("flux", e, s["flux_out"], slab + 1)

    def wave_copy(e):
        return slab_copy("right_wave", e, wave_ref, slab - 1)

    def gather_layer(j):
        return pltpu.make_async_remote_copy(
            src_ref=own, dst_ref=own,
            send_sem=s["layer_send"].at[j], recv_sem=s["layer_recv"].at[j],
            device_id={"energy": layer_peer(j)}, device_id_type=MESH,
        )

    def gather_across(h, i):
        axis = ("yx", "xy")[h][i]
        columns = pl.ds(h * (orbitals // 2), orbitals // 2)
        yy = y if axis == "y" or i == 0 else slice(None)
        xx = x if axis == "x" or i == 0 else slice(None)
        block = gathered.at[:, yy, xx, :, columns]
        return pltpu.make_async_remote_copy(
            src_ref=block, dst_ref=block,
            send_sem=s["across_send"].at[h, i], recv_sem=s["across_recv"].at[h, i],
            device_id={"energy": across[axis]}, device_id_type=MESH,
        )

    def gather_0():
        for j in range(1, layers):
            gather_layer(j).start()

    def gather_1():
        for j in range(1, layers):
            gather_layer(j).wait_recv()
        for h in range(2):
            gather_across(h, 0).start()

    def gather_2():
        for h in range(2):
            gather_across(h, 0).wait_recv()
            gather_across(h, 1).start()

    def gather_3():
        for h in range(2):
            gather_across(h, 1).wait_recv()
        whole = gathered[...].astype(F32).reshape(orbitals, orbitals)
        blocks = s["mask"].shape[0]
        tile = orbitals // blocks
        for i in range(blocks):
            for j in range(blocks):
                block = whole[i * tile:(i + 1) * tile, j * tile:(j + 1) * tile] * s["mask"][i, j].astype(F32)
                s["coupled"][i * tile:(i + 1) * tile, j * tile:(j + 1) * tile] = block.astype(BF16)

    def transpose_coupled():
        s["coupled_t"][...] = s["coupled"][...].T

    def send_first():
        for e in range(count):
            load([e])
            s["first"][e] = green(e, source_ref[e])
            start_copy(e).start()

    def sweep(has_left):
        gather_0()
        if has_left:
            send_first()
        else:
            load(range(1))
        gather_1()
        gather_2()
        if not has_left:
            load(range(1, count))
        gather_3()
        for e in range(count):
            start_copy(e).wait_recv()
            total = source_ref[e].astype(F32) + dot(s["coupled"][...], s["start"][e])
            if has_left:
                flux_copy(e).wait_recv()
                total = total + s["flux"][e].astype(F32)
            forward = green(e, total.astype(BF16))
            if e == 0:
                transpose_coupled()
            s["flux_out"][e] = dot(s["coupled_t"][...], forward).astype(BF16)
            flux_copy(e).start()
        for e in range(count):
            wave_copy(e).wait_recv()
            total = source_ref[e].astype(F32) + dot(s["coupled"][...], s["right_wave"][e])
            if has_left:
                total = total + s["flux"][e].astype(F32)
            wave_ref[e] = green(e, total.astype(BF16))
            if has_left:
                wave_copy(e).start()

    def last_sweep():
        send_first()
        for e in range(count):
            flux_copy(e).wait_recv()
            if e == 0:
                gather_0()
            total = source_ref[e].astype(F32) + s["flux"][e].astype(F32)
            wave_ref[e] = green(e, total.astype(BF16))
            wave_copy(e).start()
        gather_1()

    @pl.when(slab == 0)
    def _():
        sweep(False)

    if slabs > 2:
        @pl.when((slab > 0) & (slab < slabs - 1))
        def _():
            sweep(True)

    @pl.when(slab == slabs - 1)
    def _():
        last_sweep()

    chunks = 4
    width = 2 * orbitals // chunks

    def scatter_axis(c, i):
        return ("xy", "yx")[c % 2][i]

    def scatter_place(c, i, keep):
        axis = scatter_axis(c, i)
        here = (x if axis == "x" else y) if keep else (1 - x if axis == "x" else 1 - y)
        if i == 1:
            return (slice(None), here)
        return (slice(None), slice(None), here) if axis == "x" else (slice(None), here)

    def scatter_across(c, i):
        return pltpu.make_async_remote_copy(
            src_ref=s["part"][c][i].at[scatter_place(c, i, False)], dst_ref=s["part_in"][c][i],
            send_sem=s["scatter_send"].at[c, i], recv_sem=s["scatter_recv"].at[c, i],
            device_id={"energy": across[scatter_axis(c, i)]}, device_id_type=MESH,
        )

    def scatter_layer(c, j):
        return pltpu.make_async_remote_copy(
            src_ref=s["part"][c][2].at[(z + j) % layers], dst_ref=s["part_in"][c][2].at[j],
            send_sem=s["final_send"].at[c, j], recv_sem=s["final_recv"].at[c, j],
            device_id={"energy": layer_peer(j)}, device_id_type=MESH,
        )

    scaled = []
    for e in range(count):
        index = jnp.full((1, 2 * modes), s["index"][e].astype(F32), F32)
        weight = scale / (1.0 + jnp.exp((index - 128.0) / 24.0))
        scaled.append((wave_ref[e].astype(F32) * weight).astype(BF16))
    left_side = jnp.concatenate(scaled, axis=1)
    for c in range(chunks):
        imag, quarter = c % 2, c // 2
        span = slice(quarter * width, (quarter + 1) * width)
        waves = [turned(wave_ref[e, span, :]) if imag else wave_ref[e, span, :] for e in range(count)]
        part = dot_nt(left_side, jnp.concatenate(waves, axis=1))
        s["part"][c][0][...] = part.reshape(layers, 2, 2, rows, width).astype(BF16)
        scatter_across(c, 0).start()

    def outflow():
        for e in range(count):
            outflow_ref[e] = dot(s["coupled_t"][...], wave_ref[e]).astype(BF16)

    @pl.when(slab < slabs - 1)
    def _():
        outflow()

    @pl.when(slab == slabs - 1)
    def _():
        gather_2()

    for i in range(2):
        for c in range(chunks):
            scatter_across(c, i).wait_recv()
            total = s["part"][c][i][scatter_place(c, i, True)].astype(F32) + s["part_in"][c][i][...].astype(F32)
            s["part"][c][i + 1][...] = total.astype(BF16)
            if i == 0:
                scatter_across(c, 1).start()
            else:
                for j in range(1, layers):
                    scatter_layer(c, j).start()

    @pl.when(slab == slabs - 1)
    def _():
        gather_3()
        transpose_coupled()
        outflow()

    for c in range(chunks):
        imag, quarter = c % 2, c // 2
        total = s["part"][c][2][z].astype(F32)
        for j in range(1, layers):
            scatter_layer(c, j).wait_recv()
            total = total + s["part_in"][c][2][j].astype(F32)
        begin = imag * orbitals + quarter * width
        density_ref[:, begin:begin + width] = total

    for j in range(1, layers):
        gather_layer(j).wait_send()
        for c in range(chunks):
            scatter_layer(c, j).wait_send()
    for i in range(2):
        for h in range(2):
            gather_across(h, i).wait_send()
        for c in range(chunks):
            scatter_across(c, i).wait_send()

    @pl.when(slab > 0)
    def _():
        for e in range(count):
            start_copy(e).wait_send()
            wave_copy(e).wait_send()

    @pl.when(slab < slabs - 1)
    def _():
        for e in range(count):
            flux_copy(e).wait_send()


def shards(green_local, coupling, masks, incident, energy_index):
    count = green_local.shape[0]
    orbitals = green_local.shape[3]
    modes = incident.shape[4]
    rows = coupling.shape[1]
    slabs = lax.axis_size("slab")
    n = lax.axis_size("energy")
    layers = n // 4
    chunks = 4
    width = 2 * orbitals // chunks
    wave = (count, orbitals, 2 * modes)
    dma = pltpu.SemaphoreType.DMA
    scratch = {
        "gathered": pltpu.VMEM((layers, 2, 2, rows, orbitals), BF16),
        "raw": pltpu.VMEM((count, orbitals, 2, modes), BF16),
        "source": pltpu.VMEM(wave, BF16),
        "index": pltpu.SMEM((count,), jnp.int32),
        "mask": pltpu.SMEM(masks.shape[1:], jnp.int32),
        "green": pltpu.VMEM((count, orbitals, 2 * orbitals), BF16),
        "coupled": pltpu.VMEM((orbitals, orbitals), BF16),
        "coupled_t": pltpu.VMEM((orbitals, orbitals), BF16),
        "first": pltpu.VMEM(wave, BF16),
        "flux_out": pltpu.VMEM(wave, BF16),
        "part": [[pltpu.VMEM((layers,) + (2,) * (2 - i) + (rows, width), BF16) for i in range(3)] for c in range(chunks)],
        "part_in": [[pltpu.VMEM((layers,) + (2,) * max(1 - i, 0) + (rows, width), BF16) for i in range(3)] for c in range(chunks)],
        "local": dma((4,)),
        "green_in": dma((count, 2)),
        "layer_send": dma((layers,)),
        "layer_recv": dma((layers,)),
        "across_send": dma((2, 2)),
        "across_recv": dma((2, 2)),
        "scatter_send": dma((chunks, 2)),
        "scatter_recv": dma((chunks, 2)),
        "final_send": dma((chunks, layers)),
        "final_recv": dma((chunks, layers)),
    }
    for name in ("start", "flux", "right_wave"):
        scratch[name] = pltpu.VMEM(wave, BF16)
        scratch[name + "_send"] = dma((count, PIECES))
        scratch[name + "_recv"] = dma((count, PIECES))
    vmem = pl.BlockSpec(memory_space=pltpu.VMEM)
    hbm = pl.BlockSpec(memory_space=pltpu.HBM)
    wave_field, outflow, density = pl.pallas_call(
        functools.partial(build, n, slabs, count, 4.0 / (count * n * modes)),
        out_shape=(
            pltpu.VMEM(wave, BF16),
            pltpu.VMEM(wave, BF16),
            pltpu.VMEM((rows, 2 * orbitals), F32),
        ),
        in_specs=[hbm] * 5,
        out_specs=(vmem, vmem, vmem),
        scratch_shapes=[scratch],
        compiler_params=pltpu.CompilerParams(
            collective_id=0, has_side_effects=True, vmem_limit_bytes=60 * 2**20
        ),
        name="sweep_and_density",
    )(energy_index, masks, green_local, incident, coupling)
    shape = (count, 1, orbitals, 2, modes)
    return (wave_field.reshape(shape), outflow.reshape(shape), density.reshape(1, rows, 2, orbitals))


def solution(mesh):
    return jax.shard_map(
        shards,
        mesh=mesh,
        in_specs=(
            P("energy", "slab", None, None, None),
            P("slab", "energy", None),
            P("slab", None, None),
            P("energy", "slab", None, None, None),
            P("energy"),
        ),
        out_specs=(
            P("energy", "slab", None, None, None),
            P("energy", "slab", None, None, None),
            P("slab", "energy", None, None),
        ),
        check_vma=False,
    )
```
